128 devices in a mesh: tp: 4 (over z_lo, core), cp: 32 (over x, z_hi, y).
Axes of the slice: x: 4, y: 4, z: 4 (z_hi: 2, z_lo: 2; z = z_hi * 2 + z_lo), core: 2. Of those that a mesh axis runs over, the one named last changes fastest.
Arguments:
- grad_out: bfloat16 [4, 4096, 4096], P('tp', 'cp'), may hold values from -6 to 6
- expert_ids: int32 [4, 4096, 8], P('tp', 'cp'), may hold values from 0 to 127, all different within a row; in each aligned block of 128 rows (0 to 127, 128 to 255, ..., all dimensions but the last counted through in order) at most 10 rows name the same one
- route_prob: bfloat16 [4, 4096, 8], P('tp', 'cp'), may hold values from 0.049804688 to 0.5
- attn_out: bfloat16 [16384, 4096], P('cp', 'tp'), may hold values from -0.046875 to 0.046875
- w_down: bfloat16 [128, 768, 4096], P(('tp', 'cp')), may hold values from -0.09375 to 0.09375
- hidden_saved: bfloat16 [128, 1280, 768], P(('tp', 'cp')), may hold values from -0.21875 to 0.21875
Outputs:
- grad_prob: float32 [4, 4096, 8], P('tp', 'cp')
- grad_hidden: bfloat16 [128, 1280, 768], P(('tp', 'cp'))
- grad_down: bfloat16 [128, 768, 4096], P(('tp', 'cp'))
- grad_oproj: bfloat16 [4096, 4096], P('cp', 'tp')
The draws below stay inside these ranges and needn't reach their ends.
Inputs may be any that keep to these rules, and one draw needn't show every extreme that they name: `expert_ids`: within each device's block of 128 tokens, no expert is named by more than 10 routes, and in every draw some expert is named by exactly 10; every expert is named somewhere.
All inputs are finite; a program needn't handle non-finite values.
Results may differ from the reference program's by a relative error of at most 0.0049.
Values may be sent and summed in bfloat16 or wider, within the bound.
No kernel may reach another device: no remote copies, remote signals or barrier semaphores. Data moves between devices by JAX's collectives and lax.ppermute only.
A program may use at most 192 MiB of HBM per device.

```python
import math
import jax
import jax.numpy as jnp
import numpy as np
from jax import lax

D = 4096
HID = 768
TOP = 8
TOK_DEV = 128
EXPERTS = 128
CAP = 10
SLOTS = 1280
HQD = 4096
CTX = 4096
TOKENS = 16384
N_TP = 4
N_CP = 32


def levels(stream_key, dims, split, low, high):
    level = 1.0
    for dim, blocks in split:
        draws = jax.random.uniform(jax.random.fold_in(jax.random.fold_in(stream_key, 6), dim), (blocks,), jnp.float32, low / len(split), high / len(split))
        level = level * jnp.repeat(jnp.exp(draws), dims[dim] // blocks).reshape((-1,) + (1,) * (len(dims) - 1 - dim))
    return level


def shared_out(key, own, number, rows, number_of, top, bound, lean):
    ranking = jax.random.permutation(key, number_of)
    crowded, usual = shares(number_of, rows * top, bound, lean, True), shares(number_of, rows * top, bound, lean, False)
    places = jnp.arange(number_of)

    def named(sizes, rotation):
        used = int((sizes > 0).sum())
        fixed = max(1, used // 4)
        moved = fixed + (places - fixed + rotation * (used - fixed)) % max(1, number_of - fixed)
        return jnp.zeros((number_of,), jnp.int32).at[ranking[jnp.where(places < fixed, places, moved)]].set(jnp.asarray(sizes, jnp.int32))

    sizes = jnp.where(number % 4 == 0, named(crowded, number // 4), named(usual, number - number // 4 - 1))
    mixed = jax.random.permutation(jax.random.fold_in(own, 3), number_of)
    giver, sink = mixed[0:number_of // 2 * 2:2], mixed[1:number_of // 2 * 2:2]
    room = jnp.minimum(sizes[giver] - 1, bound - sizes[sink]) // 2
    room = jnp.where((giver == ranking[0]) | (sink == ranking[0]) | (sizes[sink] == 0), 0, jnp.maximum(room, 0))
    moved = jax.random.randint(jax.random.fold_in(own, 4), (number_of // 2,), 0, 1 << 20) % (room + 1)
    sizes = sizes.at[giver].add(-moved).at[sink].add(moved)
    labels = jnp.searchsorted(jnp.cumsum(sizes), jnp.arange(rows * top), side="right").astype(jnp.int32)
    table = labels.reshape(top, rows).T
    table = table[jax.random.permutation(jax.random.fold_in(own, 1), rows)]
    rotation = jax.random.randint(jax.random.fold_in(own, 2), (rows, 1), 0, top)
    return jnp.take_along_axis(table, (jnp.arange(top)[None, :] + rotation) % top, axis=1)


def shares(count, total, bound, slope, full):
    loads = [(1 << 20) // math.isqrt(rank ** slope) + 1 for rank in range(1, count + 1)]
    largest = bound if full else min(bound, max(-(-total // count), total * loads[0] // sum(loads)))
    least = 1 if total - largest >= count - 1 else 0
    given, surplus = [largest] + [least] * (count - 1), total - largest - least * (count - 1)
    while surplus > 0:
        candidates = [i for i in range(1, count) if given[i] < largest] or [i for i in range(1, count) if given[i] < bound]
        whole, left = sum([loads[i] for i in candidates]), surplus
        for i in candidates:
            more = min(bound - given[i], max(1, left * loads[i] // whole), surplus)
            given[i] = given[i] + more
            surplus = surplus - more
    return np.array(given)


def bell_draw(own_key, dims, width, most, split=(), kind=jnp.bfloat16):
    entries = jax.random.normal(own_key, dims, jnp.float32) * width
    if len(split) > 0:
        entries = levels(own_key, dims, split, -0.22, 0.18) * entries
    return jnp.clip(entries, min=-most, max=most).astype(kind)


def setup_inputs(seed: int = 0) -> dict:
    seeds = jax.random.split(jax.random.key(seed), 7)
    grad_out = bell_draw(seeds[0], (N_TP, CTX, D), 1.0, 6.0, ((0, 4), (1, 32)))
    expert_ids_keys = jax.random.split(jax.random.fold_in(seeds[1], 1), N_TP * CTX // TOK_DEV)
    expert_ids_turns = jax.random.permutation(jax.random.fold_in(seeds[1], 3), N_TP * CTX // TOK_DEV)
    expert_ids = jax.vmap(lambda own, number: shared_out(jax.random.fold_in(seeds[1], 2), own, number, TOK_DEV, N_TP * N_CP, TOP, CAP, 2))(expert_ids_keys, expert_ids_turns).reshape((N_TP, CTX, TOP))
    route_prob = jnp.clip(0.049804688 + 0.4501953 * jax.random.uniform(seeds[2], (N_TP, CTX, TOP), jnp.float32) ** levels(seeds[2], (N_TP, CTX, TOP), ((0, 4), (1, 32)), -0.2, 0.2), 0.049804688, 0.5).astype(jnp.bfloat16)
    attn_out = bell_draw(seeds[3], (TOKENS, HQD), TOKENS ** -0.5, 0.046875, ((0, 32), (1, 4)))
    w_down = bell_draw(seeds[4], (EXPERTS, HID, D), D ** -0.5, 0.09375, ((0, 128),))
    hidden_saved = bell_draw(seeds[5], (EXPERTS, SLOTS, HID), HID ** -0.5, 0.21875, ((0, 128),))
    return {"grad_out": grad_out, "expert_ids": expert_ids, "route_prob": route_prob, "attn_out": attn_out, "w_down": w_down, "hidden_saved": hidden_saved}


def reference(grad_out, expert_ids, route_prob, attn_out, w_down, hidden_saved):
    n_experts = N_TP * N_CP
    per_block = TOK_DEV * TOP
    block_ids = expert_ids.reshape(n_experts, per_block)
    onehot = (block_ids[:, :, None] == jnp.arange(n_experts, dtype=jnp.int32)[None, None, :]).astype(jnp.int32)
    position = jnp.sum((jnp.cumsum(onehot, axis=1) - 1) * onehot, axis=2)
    slot_of = (jnp.arange(n_experts, dtype=jnp.int32)[:, None] * CAP + position).reshape(-1).astype(jnp.int32)
    flat_ids = block_ids.reshape(-1)
    token_of = (jnp.arange(n_experts * per_block, dtype=jnp.int32) // TOP).astype(jnp.int32)
    rows_all = grad_out.reshape(-1, D)
    probs_all = route_prob.reshape(-1).astype(jnp.float32)

    def per_expert(expert):
        target = jnp.where(flat_ids == expert, slot_of, SLOTS).astype(jnp.int32)
        source = jnp.zeros((SLOTS + 1,), jnp.int32).at[target].set(token_of)[:SLOTS]
        live = jnp.zeros((SLOTS + 1,), jnp.float32).at[target].set(1.0)[:SLOTS]
        weight = jnp.zeros((SLOTS + 1,), jnp.float32).at[target].set(probs_all)[:SLOTS]
        routed = jnp.where(live[:, None] > 0.5, rows_all[source], jnp.zeros((), jnp.bfloat16)).astype(jnp.bfloat16)
        proj = jnp.dot(routed, w_down[expert].T, preferred_element_type=jnp.float32)
        grad_hid = (weight[:, None] * proj).astype(jnp.bfloat16)
        prob_part = jnp.sum(proj * hidden_saved[expert].astype(jnp.float32), axis=1)
        weighted = (weight[:, None] * routed.astype(jnp.float32)).astype(jnp.bfloat16)
        grad_w = jnp.dot(hidden_saved[expert].T, weighted, preferred_element_type=jnp.float32).astype(jnp.bfloat16)
        return grad_hid, prob_part, grad_w

    grad_hidden, prob_parts, grad_down = lax.map(per_expert, jnp.arange(n_experts, dtype=jnp.int32))
    lookup = (flat_ids * SLOTS + slot_of).astype(jnp.int32)
    grad_prob = prob_parts.reshape(-1)[lookup].reshape(N_TP, CTX, TOP)
    ordered = grad_out.reshape(N_TP, N_CP, TOK_DEV, D).transpose(1, 0, 2, 3).reshape(TOKENS, D)
    grad_oproj = jnp.dot(ordered.T, attn_out, preferred_element_type=jnp.float32).astype(jnp.bfloat16)
    return grad_prob, grad_hidden, grad_down, grad_oproj
```

```python
import jax
import jax.numpy as jnp
from jax import lax
from jax.experimental import pallas as pl
from jax.experimental.pallas import tpu as pltpu
from jax.sharding import Mesh
from jax.sharding import PartitionSpec as P

TP = ("zlo", "core")
CP = ("x", "zhi", "y")
ALL = TP + CP
PEERS = ("zlo", "core", "x", "zhi")
CHUNKS = 2
TILE = 512
VMEM = 56 * 1024 * 1024
BF = jnp.bfloat16
F32 = jnp.float32


def params():
    return pltpu.CompilerParams(vmem_limit_bytes=VMEM)


def upper(n):
    return (
        lax.broadcasted_iota(jnp.int32, (n, n), 0) < lax.broadcasted_iota(jnp.int32, (n, n), 1)
    ).astype(BF)


def ranks(member):
    count = jnp.dot(member.astype(BF), upper(member.shape[1]), preferred_element_type=F32)
    return jnp.where(member, count, -1.0)


def place_kernel(y_ref, ids_ref, s_ref):
    y = y_ref[0]
    rows, cols = s_ref.shape
    peers = rows // 40
    expert = lax.broadcasted_iota(jnp.int32, (peers, 128), 0) * 4 + y
    parts = []
    for k in range(4):
        member = ids_ref[k, 0:1, :] == expert
        for i in range(1, 8):
            member = member | (ids_ref[k, i : i + 1, :] == expert)
        parts.append(ranks(member).astype(BF))
    table = jnp.concatenate(parts, axis=1)
    row = lax.broadcasted_iota(jnp.int32, (rows, peers), 0)
    pick = (lax.shift_right_logical(row * 6554, 18) == lax.broadcasted_iota(jnp.int32, (rows, peers), 1)).astype(BF)
    spread = jnp.dot(pick, table, preferred_element_type=F32)
    row = lax.broadcasted_iota(jnp.int32, (rows, cols), 0)
    tenth = lax.shift_right_logical(row * 6554, 16)
    rank = (row - tenth * 10).astype(F32)
    block = lax.shift_right_logical(lax.broadcasted_iota(jnp.int32, (rows, cols), 1), 7)
    origin = jnp.where(block == 0, 0, jnp.where(block == 1, 3, jnp.where(block == 2, 1, 2)))
    here = (tenth & 3) == ((origin + y) & 3)
    s_ref[...] = jnp.where(here & (spread == rank), 1.0, 0.0).astype(BF)


def place(y, ids4, rows):
    return pl.pallas_call(
        place_kernel,
        out_shape=jax.ShapeDtypeStruct((rows, 512), BF),
        in_specs=[
            pl.BlockSpec(memory_space=pltpu.SMEM),
            pl.BlockSpec(memory_space=pltpu.VMEM),
        ],
        out_specs=pl.BlockSpec(memory_space=pltpu.VMEM),
        compiler_params=params(),
        cost_estimate=pl.CostEstimate(flops=10**8, bytes_accessed=2 * 10**6, transcendentals=0),
    )(y, ids4)


def dispatch_kernel(s_ref, g0, g1, g2, g3, g4, o_ref):
    g = jnp.concatenate([g0[...], g1[...], g2[...], g3[...], g4[...]], axis=0)
    o_ref[...] = jnp.dot(s_ref[...], g, preferred_element_type=F32).astype(BF)


def dispatch(s, blocks):
    rows = s.shape[0]
    width = blocks[0].shape[1]
    return pl.pallas_call(
        dispatch_kernel,
        out_shape=jax.ShapeDtypeStruct((rows, width), BF),
        grid=(width // TILE,),
        in_specs=[pl.BlockSpec(s.shape, lambda i: (0, 0))]
        + [pl.BlockSpec((b.shape[0], TILE), lambda i: (0, i)) for b in blocks],
        out_specs=pl.BlockSpec((rows, TILE), lambda i: (0, i)),
        compiler_params=params(),
        cost_estimate=pl.CostEstimate(
            flops=2 * rows * 512 * width, bytes_accessed=2 * rows * width, transcendentals=0
        ),
    )(s, *blocks)


def select_kernel(y_ref, *refs):
    o_ref = refs[-1]
    y = y_ref[0]
    for ref, shift, start in zip(refs[:-1], (0, 3, 1, 2, 2), (0, 0, 0, 0, 64)):
        at = pl.multiple_of(((y + shift) & 3) * 128 + start, 64)
        o_ref[pl.ds(at, ref.shape[0]), :] = ref[...]


def select(y, blocks):
    width = blocks[0].shape[1]
    n = width // 512
    return pl.pallas_call(
        select_kernel,
        out_shape=jax.ShapeDtypeStruct((512, n * 128), BF),
        grid_spec=pltpu.PrefetchScalarGridSpec(
            num_scalar_prefetch=1,
            grid=(n,),
            in_specs=[
                pl.BlockSpec((b.shape[0], 128), lambda i, y_ref: (0, i * 4 + y_ref[0])) for b in blocks
            ],
            out_specs=pl.BlockSpec((512, 128), lambda i, y_ref: (0, i)),
        ),
        compiler_params=params(),
        cost_estimate=pl.CostEstimate(flops=0, bytes_accessed=4 * 512 * n * 128, transcendentals=0),
    )(y, *blocks)


def expert_kernel(first, last, *refs):
    if first:
        routed_ref, w_ref, ht_ref, wt_ref = refs[:4]
        outs = refs[4:]
    else:
        routed_ref, w_ref, ht_ref, wt_ref, before_ref, h_ref = refs[:6]
        outs = refs[7:]
    step = pl.program_id(0)
    if last:
        down_ref, hid_ref, part_ref, proj_ref = outs
    else:
        down_ref, proj_ref = outs
    routed = routed_ref[...]
    term = lax.dot_general(
        routed, w_ref[...], (((1,), (1,)), ((), ())), preferred_element_type=F32
    )

    @pl.when(step == 0)
    def _():
        if first:
            proj_ref[...] = term
        else:
            proj_ref[...] = before_ref[...] + term

    @pl.when(step > 0)
    def _():
        proj_ref[...] += term

    weighted = (wt_ref[...] * routed.astype(F32)).astype(BF)
    down_ref[...] = jnp.dot(ht_ref[...], weighted, preferred_element_type=F32).astype(BF)
    if last:

        @pl.when(step == pl.num_programs(0) - 1)
        def _():
            proj = proj_ref[...]
            hid_ref[...] = (wt_ref[...] * proj).astype(BF)
            part_ref[...] = jnp.sum(proj * h_ref[...].astype(F32), axis=1, keepdims=True)


def expert(chunk, n_chunks, routed, w, hidden_t, weight, proj, hidden, down):
    rows, width = routed.shape
    hid, full = w.shape
    first, last = chunk == 0, chunk == n_chunks - 1
    steps = width // TILE
    base = chunk * steps
    in_specs = [
        pl.BlockSpec((rows, TILE), lambda i: (0, i)),
        pl.BlockSpec((hid, TILE), lambda i: (0, base + i)),
        pl.BlockSpec((hid, rows), lambda i: (0, 0)),
        pl.BlockSpec((rows, 1), lambda i: (0, 0)),
    ]
    args = [routed, w, hidden_t, weight]
    aliases = {}
    if not first:
        in_specs += [
            pl.BlockSpec((rows, hid), lambda i: (0, 0)),
            pl.BlockSpec((rows, hid), lambda i: (0, 0)),
            pl.BlockSpec(memory_space=pl.ANY),
        ]
        args += [proj, hidden, down]
        aliases = {6: 0}
    out_shape = [jax.ShapeDtypeStruct((hid, full), BF)]
    out_specs = [pl.BlockSpec((hid, TILE), lambda i: (0, base + i))]
    scratch = []
    whole = lambda i: (0, 0)
    if last:
        out_shape += [jax.ShapeDtypeStruct((rows, hid), BF), jax.ShapeDtypeStruct((rows, 1), F32)]
        out_specs += [pl.BlockSpec((rows, hid), whole), pl.BlockSpec((rows, 1), whole)]
        scratch = [pltpu.VMEM((rows, hid), F32)]
    else:
        out_shape += [jax.ShapeDtypeStruct((rows, hid), F32)]
        out_specs += [pl.BlockSpec((rows, hid), whole)]

    def kernel(*refs):
        expert_kernel(first, last, *refs)

    return pl.pallas_call(
        kernel,
        out_shape=out_shape,
        grid=(steps,),
        in_specs=in_specs,
        out_specs=out_specs,
        scratch_shapes=scratch,
        input_output_aliases=aliases,
        compiler_params=params(),
        cost_estimate=pl.CostEstimate(
            flops=4 * rows * hid * width, bytes_accessed=2 * (rows + 2 * hid) * width, transcendentals=0
        ),
    )(*args)


def ring(x, shift):
    return lax.ppermute(x, "y", [(i, (i + shift) % 4) for i in range(4)])


def ring_gather(x):
    half = x.shape[0] // 2
    before, after = ring(x, 1), ring(x, -1)
    return [x, before, after, ring(before[:half], 1), ring(after[half:], -1)]


def local(grad_out, expert_ids, route_prob, attn_out, w_down, hidden_saved):
    n_experts = lax.axis_size(ALL)
    slots = hidden_saved.shape[1]
    cap = slots // n_experts
    g = grad_out[0]
    tokens, width = g.shape
    y = lax.axis_index("y").reshape(1)
    chunk = width // CHUNKS
    ids = expert_ids[0].T
    blocks = [ring_gather(g[:, i * chunk : (i + 1) * chunk]) for i in range(CHUNKS)]
    ids4 = jnp.stack([ids, ring(ids, 1), ring(ids, -1), ring(ids, 2)])
    spread = place(y, ids4, slots)
    named = ids[:, None, :] == jnp.arange(n_experts, dtype=jnp.int32)[None, :, None]
    rank = ranks(jnp.any(named, axis=0))
    prob = jnp.sum(jnp.where(named, route_prob[0].T[:, None, :].astype(F32), 0.0), axis=0)
    at = rank[:, None, :] == jnp.arange(cap, dtype=jnp.int32).astype(F32)[None, :, None]
    send_prob = jnp.sum(jnp.where(at, prob[:, None, :], 0.0), axis=2)
    got_prob = lax.all_to_all(
        send_prob.reshape(n_experts, 1, cap), ALL, split_axis=0, concat_axis=0, tiled=True
    )
    weight = got_prob.reshape(slots, 1)
    hidden = hidden_saved[0]
    hidden_t = hidden.T
    w = w_down[0]
    routed = []
    for part in blocks:
        rows = dispatch(spread, part)
        sent = lax.all_to_all(
            rows.reshape(n_experts // 4, 4 * cap, chunk), PEERS, split_axis=0, concat_axis=0, tiled=True
        )
        routed.append(sent.reshape(slots, chunk))
    proj = down = None
    for i in range(CHUNKS):
        out = expert(i, CHUNKS, routed[i], w, hidden_t, weight, proj, hidden, down)
        down, proj = out[0], out[-1]
    _, grad_hid, part = out
    returned = lax.all_to_all(
        part.reshape(n_experts, 1, cap), ALL, split_axis=0, concat_axis=0, tiled=True
    ).reshape(n_experts, cap)
    value = jnp.sum(jnp.where(at, returned[:, :, None], 0.0), axis=1)
    grad_prob = jnp.sum(jnp.where(named, value[None], 0.0), axis=1).T[None]

    features = jnp.concatenate([select(y, part) for part in blocks], axis=1)
    features = lax.all_gather(features, TP, axis=0, tiled=False)
    context = lax.all_gather(attn_out, "y", axis=0, tiled=False)
    context = context.reshape(4, 4, tokens, -1).transpose(1, 0, 2, 3).reshape(16 * tokens, -1)
    partial = lax.dot_general(
        features.reshape(16 * tokens, -1), context, (((0,), (0,)), ((), ())), preferred_element_type=F32
    )
    grad_oproj = lax.psum_scatter(partial, ("x", "zhi"), scatter_dimension=0, tiled=True).astype(BF)
    return (grad_prob, grad_hid[None], down[None], grad_oproj)


def solution(mesh):
    fine = Mesh(mesh.devices.reshape(2, 2, 4, 2, 4), ALL)
    in_specs = (
        P(TP, CP, None),
        P(TP, CP, None),
        P(TP, CP, None),
        P(CP, TP),
        P(ALL, None, None),
        P(ALL, None, None),
    )
    out_specs = (
        P(TP, CP, None),
        P(ALL, None, None),
        P(ALL, None, None),
        P(CP, TP),
    )
    return jax.shard_map(local, mesh=fine, in_specs=in_specs, out_specs=out_specs, check_vma=False)
```

```python
import jax
import jax.numpy as jnp
from jax import lax
from jax.experimental import pallas as pl
from jax.experimental.pallas import tpu as pltpu
from jax.sharding import Mesh
from jax.sharding import PartitionSpec as P

TP = ("zlo", "core")
CP = ("x", "zhi", "y")
ALL = TP + CP
PEERS = ("zlo", "core", "x", "zhi")
CHUNKS = ((2560, 1536), (0, 2560))
TILE = 512
WIDE = 512
VMEM = 56 * 1024 * 1024
BF = jnp.bfloat16
F32 = jnp.float32


def params():
    return pltpu.CompilerParams(vmem_limit_bytes=VMEM)


def cost(flops, moved):
    return pl.CostEstimate(flops=flops, bytes_accessed=moved, transcendentals=0)


def upper(n):
    return (
        lax.broadcasted_iota(jnp.int32, (n, n), 0) < lax.broadcasted_iota(jnp.int32, (n, n), 1)
    ).astype(BF)


def ranks(member):
    count = jnp.dot(member.astype(BF), upper(member.shape[1]), preferred_element_type=F32)
    return jnp.where(member, count, -1.0)


def place_kernel(y_ref, *refs):
    s_ref = refs[-1]
    y = y_ref[0]
    rows, cols = s_ref.shape
    peers = rows // 40
    expert = (lax.broadcasted_iota(jnp.int32, (peers, 128), 0) * 4 + y).astype(F32)
    parts = []
    for ref in refs[:-1]:
        named = ref[...].astype(F32)
        member = named[0:1, :] == expert
        for i in range(1, 8):
            member = member | (named[i : i + 1, :] == expert)
        parts.append(ranks(member).astype(BF))
    table = jnp.concatenate(parts, axis=1)
    row = lax.broadcasted_iota(jnp.int32, (rows, peers), 0)
    peer = lax.broadcasted_iota(jnp.int32, (rows, peers), 1)
    pick = (lax.shift_right_logical(row * 6554, 18) == peer).astype(BF)
    spread = jnp.dot(pick, table, preferred_element_type=F32)
    row = lax.broadcasted_iota(jnp.int32, (rows, cols), 0)
    tenth = lax.shift_right_logical(row * 6554, 16)
    rank = (row - tenth * 10).astype(F32)
    block = lax.shift_right_logical(lax.broadcasted_iota(jnp.int32, (rows, cols), 1), 7)
    origin = jnp.where(block == 0, 0, jnp.where(block == 1, 3, jnp.where(block == 2, 1, 2)))
    here = (tenth & 3) == ((origin + y) & 3)
    s_ref[...] = jnp.where(here & (spread == rank), 1.0, 0.0).astype(BF)


def place(y, blocks, rows):
    last = blocks[0].shape[1] // 128 - 1
    return pl.pallas_call(
        place_kernel,
        out_shape=jax.ShapeDtypeStruct((rows, 512), BF),
        grid=(1,),
        in_specs=[pl.BlockSpec(memory_space=pltpu.SMEM)]
        + [pl.BlockSpec((16, 128), lambda i: (0, last)) for _ in blocks],
        out_specs=pl.BlockSpec((rows, 512), lambda i: (0, 0)),
        compiler_params=params(),
        cost_estimate=cost(10**8, 2 * 10**6),
    )(y, *blocks)


def dispatch_kernel(s_ref, g0, g1, g2, g3, o_ref):
    g = jnp.concatenate([g0[...], g1[...], g2[...], g3[...]], axis=0)
    o_ref[...] = jnp.dot(s_ref[...], g, preferred_element_type=F32).astype(BF)


def dispatch(s, blocks, width):
    rows = s.shape[0]
    return pl.pallas_call(
        dispatch_kernel,
        out_shape=jax.ShapeDtypeStruct((rows, width), BF),
        grid=(width // TILE,),
        in_specs=[pl.BlockSpec(s.shape, lambda i: (0, 0))]
        + [pl.BlockSpec((128, TILE), lambda i: (0, i)) for _ in blocks],
        out_specs=pl.BlockSpec((rows, TILE), lambda i: (0, i)),
        compiler_params=params(),
        cost_estimate=cost(2 * rows * 512 * width, 2 * rows * width),
    )(s, *blocks)


def select_kernel(y_ref, *refs):
    out = refs[-1]
    col = 0
    for first, (_, width) in ((4, CHUNKS[1]), (0, CHUNKS[0])):
        for i in range(width // 512):
            at = pl.multiple_of(i * 512 + y_ref[0] * 128, 128)
            for k in range(4):
                out[k * 128 : (k + 1) * 128, col : col + 128] = refs[first + k][:, pl.ds(at, 128)]
            col += 128


def select(y, low, high, width):
    moved = 8 * 128 * width
    return pl.pallas_call(
        select_kernel,
        out_shape=jax.ShapeDtypeStruct((512, width // 4), BF),
        in_specs=[pl.BlockSpec(memory_space=pltpu.SMEM)]
        + [pl.BlockSpec(memory_space=pltpu.VMEM)] * 8,
        out_specs=pl.BlockSpec(memory_space=pltpu.VMEM),
        compiler_params=params(),
        cost_estimate=cost(0, moved),
    )(y, *low, *high)


def quarter_kernel(y_ref, g_ref, *outs):
    for out, shift in zip(outs, (0, 1, 3, 2)):
        y = (y_ref[0] + shift) & 3
        for i in range(g_ref.shape[1] // 512):
            at = pl.multiple_of(i * 512 + y * 128, 128)
            out[:, i * 128 : (i + 1) * 128] = g_ref[:, pl.ds(at, 128)]


def quarters(y, g):
    return pl.pallas_call(
        quarter_kernel,
        out_shape=[jax.ShapeDtypeStruct((128, g.shape[1] // 4), BF)] * 4,
        in_specs=[pl.BlockSpec(memory_space=pltpu.SMEM), pl.BlockSpec(memory_space=pltpu.VMEM)],
        out_specs=[pl.BlockSpec(memory_space=pltpu.VMEM)] * 4,
        compiler_params=params(),
        cost_estimate=cost(0, 4 * g.shape[0] * g.shape[1]),
    )(y, g)


def outer_kernel(t_ref, *refs):
    features, contexts, (o_ref, ft, at) = refs[:4], refs[4:9], refs[9:]

    @pl.when(pl.program_id(0) == 0)
    def _():
        for i, f in enumerate(features):
            ft[:, i * 512 : (i + 1) * 512] = f[...].T

    for i in range(4):
        who = t_ref[0] ^ i
        start = pl.multiple_of(who * 128, 128)
        for k in range(3):
            at[(i * 4 + k) * 128 : (i * 4 + k + 1) * 128, :] = contexts[k][pl.ds(start, 128), :]
        start = pl.multiple_of((who & 1) * 128, 128)
        at[(i * 4 + 3) * 128 : (i * 4 + 4) * 128, :] = jnp.where(
            who < 2, contexts[3][pl.ds(start, 128), :], contexts[4][pl.ds(start, 128), :]
        )
    o_ref[...] = jnp.dot(ft[...], at[...], preferred_element_type=F32).astype(BF)


def outer(t, features, contexts):
    n, wide = features[0].shape[1], contexts[0].shape[1]
    return pl.pallas_call(
        outer_kernel,
        out_shape=jax.ShapeDtypeStruct((n, wide), BF),
        grid=(wide // 256,),
        in_specs=[pl.BlockSpec(memory_space=pltpu.SMEM)]
        + [pl.BlockSpec((512, n), lambda i: (0, 0)) for _ in features]
        + [pl.BlockSpec((c.shape[0], 256), lambda i: (0, i)) for c in contexts],
        out_specs=pl.BlockSpec((n, 256), lambda i: (0, i)),
        scratch_shapes=[pltpu.VMEM((n, 2048), BF), pltpu.VMEM((2048, 256), BF)],
        compiler_params=params(),
        cost_estimate=cost(2 * 2048 * n * wide, 2 * (4096 * n + n * wide)),
    )(t, *features, *contexts)


def proj_kernel(first, last, *refs):
    routed_ref, *refs = refs
    term = None
    tile = refs[0].shape[1]
    for i in range(routed_ref.shape[1] // tile):
        piece = lax.dot_general(
            routed_ref[:, i * tile : (i + 1) * tile],
            refs.pop(0)[...],
            (((1,), (1,)), ((), ())),
            preferred_element_type=F32,
        )
        term = piece if term is None else term + piece
    if not first:
        term = refs[0][...] + term
    if not last:
        refs[-1][...] = term
        return
    h_ref, wt_ref, hid_ref, part_ref = refs[-4:]
    hid_ref[...] = (wt_ref[...] * term).astype(BF)
    part_ref[...] = jnp.sum(term * h_ref[...].astype(F32), axis=1, keepdims=True)


def project(chunk, routed, w, before, hidden, weight):
    rows, width = routed.shape
    hid = w.shape[0]
    first, last = chunk == 0, chunk == len(CHUNKS) - 1
    tile = 256
    across = pl.BlockSpec((tile, hid), lambda i: (i, 0))
    narrow = pl.BlockSpec((tile, 1), lambda i: (i, 0))
    deep = WIDE if CHUNKS[chunk][0] else width
    start, n = CHUNKS[chunk][0] // deep, width // deep
    in_specs = [pl.BlockSpec((tile, width), lambda i: (i, 0))]
    in_specs += [pl.BlockSpec((hid, deep), lambda i, j=j: (0, j)) for j in range(start, start + n)]
    args = [routed] + [w] * n
    if not first:
        in_specs.append(across)
        args.append(before)
    if last:
        in_specs += [across, narrow]
        args += [hidden, weight]
        out_shape = [jax.ShapeDtypeStruct((rows, hid), BF), jax.ShapeDtypeStruct((rows, 1), F32)]
        out_specs = [across, narrow]
    else:
        out_shape, out_specs = jax.ShapeDtypeStruct((rows, hid), F32), across

    def kernel(*refs):
        proj_kernel(first, last, *refs)

    return pl.pallas_call(
        kernel,
        out_shape=out_shape,
        grid=(rows // tile,),
        in_specs=in_specs,
        out_specs=out_specs,
        compiler_params=params(),
        cost_estimate=cost(2 * rows * hid * width, 2 * (rows + hid) * width),
    )(*args)


def down_kernel(routed_ref, ht_ref, wt_ref, *refs):
    weighted = (wt_ref[...] * routed_ref[...].astype(F32)).astype(BF)
    refs[-1][...] = jnp.dot(ht_ref[...], weighted, preferred_element_type=F32).astype(BF)


def weigh(chunk, routed, hidden_t, weight, full, before):
    rows, width = routed.shape
    hid = hidden_t.shape[0]
    steps = width // WIDE
    base = CHUNKS[chunk][0] // WIDE
    in_specs = [
        pl.BlockSpec((rows, WIDE), lambda i: (0, i)),
        pl.BlockSpec((hid, rows), lambda i: (0, 0)),
        pl.BlockSpec((rows, 1), lambda i: (0, 0)),
    ]
    args = [routed, hidden_t, weight]
    if before is not None:
        in_specs.append(pl.BlockSpec(memory_space=pl.ANY))
        args.append(before)
    return pl.pallas_call(
        down_kernel,
        out_shape=jax.ShapeDtypeStruct((hid, full), BF),
        grid=(steps,),
        in_specs=in_specs,
        out_specs=pl.BlockSpec((hid, WIDE), lambda i: (0, base + i)),
        input_output_aliases={} if before is None else {3: 0},
        compiler_params=params(),
        cost_estimate=cost(2 * rows * hid * width, 2 * (rows + hid) * width),
    )(*args)


def ring(x, shift, axis="y", n=4):
    return lax.ppermute(x, axis, [(i, (i + shift) % n) for i in range(n)])


def swap(x, axis):
    return ring(x, 1, axis, 2)


def ring_gather(x):
    return [x, ring(x, 1), ring(x, -1), ring(x, 2)]


def after(x, *others):
    return lax.optimization_barrier((x, *others))[0]


def local(grad_out, expert_ids, route_prob, attn_out, w_down, hidden_saved):
    n_experts = lax.axis_size(ALL)
    slots = hidden_saved.shape[1]
    cap = slots // n_experts
    g = grad_out[0]
    width = g.shape[1]
    y = lax.axis_index("y").reshape(1)
    (at_near, near), (at_far, far) = CHUNKS
    ids = expert_ids[0].T
    label = jnp.pad(ids.astype(BF), ((0, g.shape[0] - ids.shape[0]), (0, 0)))
    low = ring_gather(jnp.concatenate([g[:, at_near : at_near + near], label], axis=1))
    across = swap(g, "zlo")
    spread = place(y, low, slots)
    named = ids[:, None, :] == jnp.arange(n_experts, dtype=jnp.int32)[None, :, None]
    rank = ranks(jnp.any(named, axis=0))
    prob = jnp.sum(jnp.where(named, route_prob[0].T[:, None, :].astype(F32), 0.0), axis=0)
    at = rank[:, None, :] == jnp.arange(cap, dtype=jnp.int32).astype(F32)[None, :, None]
    send_prob = jnp.sum(jnp.where(at, prob[:, None, :], 0.0), axis=2)
    got_prob = lax.all_to_all(
        send_prob.reshape(n_experts, 1, cap), ALL, split_axis=0, concat_axis=0, tiled=True
    )
    high = ring_gather(after(g[:, at_far : at_far + far], send_prob))
    *low, got_prob, across = lax.optimization_barrier((*low, got_prob, across))

    def send(rows):
        return lax.all_to_all(
            rows.reshape(n_experts // 4, 4 * cap, -1), PEERS, split_axis=0, concat_axis=0, tiled=True
        ).reshape(slots, -1)

    rows0 = dispatch(spread, low, near)
    routed0 = send(rows0)
    contexts = after(attn_out, high[3])
    contexts = [contexts, ring(contexts, 1), ring(contexts, -1)]
    parts = quarters(y, across)
    other = [ring(q, shift) if shift else q for q, shift in zip(parts, (0, 1, -1, 2))]
    mine = select(y, low, high, width)
    other = jnp.concatenate(other, axis=0)
    features = [mine, swap(mine, "core"), other, swap(other, "core")]
    rows1 = dispatch(spread, high, far)
    routed1 = send(rows1)
    t = (lax.axis_index("zlo") * 2 + lax.axis_index("core")).reshape(1)
    half = attn_out.shape[0] // 2
    contexts += [ring(contexts[1][:half], 1), ring(contexts[2][half:], -1)]
    partial = outer(t, features, contexts)

    weight = got_prob.reshape(slots, 1)
    hidden = hidden_saved[0]
    hidden_t = hidden.T
    w = w_down[0]
    x = lax.axis_index("x")
    quarter = partial.shape[0] // 4

    def piece(shift):
        return lax.dynamic_slice_in_dim(partial, ((x + shift) & 3) * quarter, quarter, 0)

    pieces = [ring(piece(shift), shift, "x") for shift in (1, -1, 2)]
    proj = project(0, routed0, w, None, hidden, weight)
    down = weigh(0, routed0, hidden_t, weight, width, None)
    grad_hid, part = project(1, routed1, w, proj, hidden, weight)
    part = part.reshape(n_experts, 1, cap)
    *pieces, part = lax.optimization_barrier((*pieces, part))
    sums = piece(0).astype(F32)
    for got in pieces:
        sums = sums + got.astype(F32)
    zhi = lax.axis_index("zhi")
    eighth = quarter // 2
    give = lax.dynamic_slice_in_dim(sums, (1 - zhi) * eighth, eighth, 0).astype(BF)
    keep = lax.dynamic_slice_in_dim(sums, zhi * eighth, eighth, 0)
    grad_oproj = (keep + swap(give, "zhi").astype(F32)).astype(BF)
    down = weigh(1, routed1, hidden_t, weight, width, down)
    returned = lax.all_to_all(
        part, ALL, split_axis=0, concat_axis=0, tiled=True
    ).reshape(n_experts, cap)
    value = jnp.sum(jnp.where(at, returned[:, :, None], 0.0), axis=1)
    grad_prob = jnp.sum(jnp.where(named, value[None], 0.0), axis=1).T[None]
    return (grad_prob, grad_hid[None], down[None], grad_oproj)


def solution(mesh):
    fine = Mesh(mesh.devices.reshape(2, 2, 4, 2, 4), ALL)
    in_specs = (
        P(TP, CP, None),
        P(TP, CP, None),
        P(TP, CP, None),
        P(CP, TP),
        P(ALL, None, None),
        P(ALL, None, None),
    )
    out_specs = (
        P(TP, CP, None),
        P(ALL, None, None),
        P(ALL, None, None),
        P(CP, TP),
    )
    return jax.shard_map(local, mesh=fine, in_specs=in_specs, out_specs=out_specs, check_vma=False)
```

```python
import jax
import jax.numpy as jnp
from jax import lax
from jax.experimental import pallas as pl
from jax.experimental.pallas import tpu as pltpu
from jax.sharding import Mesh
from jax.sharding import PartitionSpec as P

TP = ("zlo", "core")
CP = ("x", "zhi", "y")
ALL = TP + CP
PEERS = ("zlo", "core", "x", "zhi")
CHUNKS = ((2560, 1536), (0, 2560))
TILE = 512
WIDE = 512
VMEM = 56 * 1024 * 1024
BF = jnp.bfloat16
F32 = jnp.float32


def params():
    return pltpu.CompilerParams(vmem_limit_bytes=VMEM)


def cost(flops, moved):
    return pl.CostEstimate(flops=flops, bytes_accessed=moved, transcendentals=0)


def upper(n):
    return (
        lax.broadcasted_iota(jnp.int32, (n, n), 0) < lax.broadcasted_iota(jnp.int32, (n, n), 1)
    ).astype(BF)


def ranks(member):
    count = jnp.dot(member.astype(BF), upper(member.shape[1]), preferred_element_type=F32)
    return jnp.where(member, count, -1.0)


def place_kernel(y_ref, *refs):
    s_ref = refs[-1]
    y = y_ref[0]
    rows, cols = s_ref.shape
    peers = rows // 40
    expert = (lax.broadcasted_iota(jnp.int32, (peers, 128), 0) * 4 + y).astype(F32)
    parts = []
    for ref in refs[:-1]:
        named = ref[...].astype(F32)
        member = named[0:1, :] == expert
        for i in range(1, 8):
            member = member | (named[i : i + 1, :] == expert)
        parts.append(ranks(member).astype(BF))
    table = jnp.concatenate(parts, axis=1)
    row = lax.broadcasted_iota(jnp.int32, (rows, peers), 0)
    peer = lax.broadcasted_iota(jnp.int32, (rows, peers), 1)
    pick = (lax.shift_right_logical(row * 6554, 18) == peer).astype(BF)
    spread = jnp.dot(pick, table, preferred_element_type=F32)
    row = lax.broadcasted_iota(jnp.int32, (rows, cols), 0)
    tenth = lax.shift_right_logical(row * 6554, 16)
    rank = (row - tenth * 10).astype(F32)
    block = lax.shift_right_logical(lax.broadcasted_iota(jnp.int32, (rows, cols), 1), 7)
    origin = jnp.where(block == 0, 0, jnp.where(block == 1, 3, jnp.where(block == 2, 1, 2)))
    here = (tenth & 3) == ((origin + y) & 3)
    s_ref[...] = jnp.where(here & (spread == rank), 1.0, 0.0).astype(BF)


def place(y, blocks, rows):
    last = blocks[0].shape[1] // 128 - 1
    return pl.pallas_call(
        place_kernel,
        out_shape=jax.ShapeDtypeStruct((rows, 512), BF),
        grid=(1,),
        in_specs=[pl.BlockSpec(memory_space=pltpu.SMEM)]
        + [pl.BlockSpec((16, 128), lambda i: (0, last)) for _ in blocks],
        out_specs=pl.BlockSpec((rows, 512), lambda i: (0, 0)),
        compiler_params=params(),
        cost_estimate=cost(10**8, 2 * 10**6),
    )(y, *blocks)


def dispatch_kernel(s_ref, g0, g1, g2, g3, o_ref):
    g = jnp.concatenate([g0[...], g1[...], g2[...], g3[...]], axis=0)
    o_ref[...] = jnp.dot(s_ref[...], g, preferred_element_type=F32).astype(BF)


def dispatch(s, blocks, width, weight=1):
    rows = s.shape[0]
    return pl.pallas_call(
        dispatch_kernel,
        out_shape=jax.ShapeDtypeStruct((rows, width), BF),
        grid=(width // TILE,),
        in_specs=[pl.BlockSpec(s.shape, lambda i: (0, 0))]
        + [pl.BlockSpec((128, TILE), lambda i: (0, i)) for _ in blocks],
        out_specs=pl.BlockSpec((rows, TILE), lambda i: (0, i)),
        compiler_params=params(),
        cost_estimate=cost(2 * rows * 512 * width * weight, 2 * rows * width),
    )(s, *blocks)


def select_kernel(y_ref, *refs):
    out = refs[-1]
    col = 0
    for first, (_, width) in ((4, CHUNKS[1]), (0, CHUNKS[0])):
        for i in range(width // 512):
            at = pl.multiple_of(i * 512 + y_ref[0] * 128, 128)
            for k in range(4):
                out[k * 128 : (k + 1) * 128, col : col + 128] = refs[first + k][:, pl.ds(at, 128)]
            col += 128


def select(y, low, high, width):
    moved = 8 * 128 * width
    return pl.pallas_call(
        select_kernel,
        out_shape=jax.ShapeDtypeStruct((512, width // 4), BF),
        in_specs=[pl.BlockSpec(memory_space=pltpu.SMEM)]
        + [pl.BlockSpec(memory_space=pltpu.VMEM)] * 8,
        out_specs=pl.BlockSpec(memory_space=pltpu.VMEM),
        compiler_params=params(),
        cost_estimate=cost(0, moved),
    )(y, *low, *high)


def quarter_kernel(y_ref, g_ref, *outs):
    for out, shift in zip(outs, (0, 1, 3, 2)):
        y = (y_ref[0] + shift) & 3
        for i in range(g_ref.shape[1] // 512):
            at = pl.multiple_of(i * 512 + y * 128, 128)
            out[:, i * 128 : (i + 1) * 128] = g_ref[:, pl.ds(at, 128)]


def quarters(y, g):
    return pl.pallas_call(
        quarter_kernel,
        out_shape=[jax.ShapeDtypeStruct((128, g.shape[1] // 4), BF)] * 4,
        in_specs=[pl.BlockSpec(memory_space=pltpu.SMEM), pl.BlockSpec(memory_space=pltpu.VMEM)],
        out_specs=[pl.BlockSpec(memory_space=pltpu.VMEM)] * 4,
        compiler_params=params(),
        cost_estimate=cost(0, 4 * g.shape[0] * g.shape[1]),
    )(y, g)


def outer_kernel(t_ref, *refs):
    features, contexts, (o_ref, ft, at) = refs[:4], refs[4:9], refs[9:]

    @pl.when(pl.program_id(0) == 0)
    def _():
        for i, f in enumerate(features):
            turned = f[...].T
            for j in range(8):
                to, of = (j % 2 * 4 + j // 2) * 128, j * 128
                ft[to : to + 128, i * 512 : (i + 1) * 512] = turned[of : of + 128]

    for i in range(4):
        who = t_ref[0] ^ i
        start = pl.multiple_of(who * 128, 128)
        for k in range(3):
            at[(i * 4 + k) * 128 : (i * 4 + k + 1) * 128, :] = contexts[k][pl.ds(start, 128), :]
        start = pl.multiple_of((who & 1) * 128, 128)
        at[(i * 4 + 3) * 128 : (i * 4 + 4) * 128, :] = jnp.where(
            who < 2, contexts[3][pl.ds(start, 128), :], contexts[4][pl.ds(start, 128), :]
        )
    o_ref[...] = jnp.dot(ft[...], at[...], preferred_element_type=F32).astype(BF)


def outer(t, features, contexts):
    n, wide = features[0].shape[1], contexts[0].shape[1]
    return pl.pallas_call(
        outer_kernel,
        out_shape=jax.ShapeDtypeStruct((n, wide), BF),
        grid=(wide // 256,),
        in_specs=[pl.BlockSpec(memory_space=pltpu.SMEM)]
        + [pl.BlockSpec((512, n), lambda i: (0, 0)) for _ in features]
        + [pl.BlockSpec((c.shape[0], 256), lambda i: (0, i)) for c in contexts],
        out_specs=pl.BlockSpec((n, 256), lambda i: (0, i)),
        scratch_shapes=[pltpu.VMEM((n, 2048), BF), pltpu.VMEM((2048, 256), BF)],
        compiler_params=params(),
        cost_estimate=cost(2 * 2048 * n * wide, 2 * (4096 * n + n * wide)),
    )(t, *features, *contexts)


def proj_kernel(first, last, *refs):
    routed_ref, *refs = refs
    term = None
    tile = refs[0].shape[1]
    for i in range(routed_ref.shape[1] // tile):
        piece = lax.dot_general(
            routed_ref[:, i * tile : (i + 1) * tile],
            refs.pop(0)[...],
            (((1,), (1,)), ((), ())),
            preferred_element_type=F32,
        )
        term = piece if term is None else term + piece
    if not first:
        term = refs[0][...] + term
    if not last:
        refs[-1][...] = term
        return
    h_ref, wt_ref, hid_ref, part_ref = refs[-4:]
    hid_ref[...] = (wt_ref[...] * term).astype(BF)
    part = jnp.sum(term * h_ref[...].astype(F32), axis=1, keepdims=True)
    rows, peers = part.shape[0], part_ref.shape[0]
    row = lax.broadcasted_iota(jnp.int32, (rows, 128), 0)
    lane = lax.broadcasted_iota(jnp.int32, (rows, 128), 1)
    tenth = lax.shift_right_logical(row * 6554, 16)
    spread = jnp.where(lane == row - tenth * 10, part, 0.0)
    peer = lax.broadcasted_iota(jnp.int32, (peers, rows), 0)
    col = lax.shift_right_logical(lax.broadcasted_iota(jnp.int32, (peers, rows), 1) * 6554, 16)
    part_ref[...] = jnp.dot(
        (peer == col).astype(F32), spread, precision=lax.Precision.HIGHEST, preferred_element_type=F32
    )


def project(chunk, routed, w, before, hidden, weight):
    rows, width = routed.shape
    hid = w.shape[0]
    first, last = chunk == 0, chunk == len(CHUNKS) - 1
    tile = 320
    across = pl.BlockSpec((tile, hid), lambda i: (i, 0))
    narrow = pl.BlockSpec((tile, 1), lambda i: (i, 0))
    deep = WIDE if CHUNKS[chunk][0] else width
    start, n = CHUNKS[chunk][0] // deep, width // deep
    in_specs = [pl.BlockSpec((tile, width), lambda i: (i, 0))]
    in_specs += [pl.BlockSpec((hid, deep), lambda i, j=j: (0, j)) for j in range(start, start + n)]
    args = [routed] + [w] * n
    if not first:
        in_specs.append(across)
        args.append(before)
    if last:
        in_specs += [across, narrow]
        args += [hidden, weight]
        out_shape = [jax.ShapeDtypeStruct((rows, hid), BF), jax.ShapeDtypeStruct((rows // 10, 128), F32)]
        out_specs = [across, pl.BlockSpec((tile // 10, 128), lambda i: (i, 0))]
    else:
        out_shape, out_specs = jax.ShapeDtypeStruct((rows, hid), F32), across

    def kernel(*refs):
        proj_kernel(first, last, *refs)

    return pl.pallas_call(
        kernel,
        out_shape=out_shape,
        grid=(rows // tile,),
        in_specs=in_specs,
        out_specs=out_specs,
        compiler_params=params(),
        cost_estimate=cost(2 * rows * hid * width, 2 * (rows + hid) * width),
    )(*args)


def down_kernel(routed_ref, ht_ref, wt_ref, *refs):
    weighted = (wt_ref[...] * routed_ref[...].astype(F32)).astype(BF)
    refs[-1][...] = jnp.dot(ht_ref[...], weighted, preferred_element_type=F32).astype(BF)


def weigh(chunk, routed, hidden_t, weight, full, before):
    rows, width = routed.shape
    hid = hidden_t.shape[0]
    steps = width // WIDE
    base = CHUNKS[chunk][0] // WIDE
    in_specs = [
        pl.BlockSpec((rows, WIDE), lambda i: (0, i)),
        pl.BlockSpec((hid, rows), lambda i: (0, 0)),
        pl.BlockSpec((rows, 1), lambda i: (0, 0)),
    ]
    args = [routed, hidden_t, weight]
    if before is not None:
        in_specs.append(pl.BlockSpec(memory_space=pl.ANY))
        args.append(before)
    return pl.pallas_call(
        down_kernel,
        out_shape=jax.ShapeDtypeStruct((hid, full), BF),
        grid=(steps,),
        in_specs=in_specs,
        out_specs=pl.BlockSpec((hid, WIDE), lambda i: (0, base + i)),
        input_output_aliases={} if before is None else {3: 0},
        compiler_params=params(),
        cost_estimate=cost(2 * rows * hid * width, 2 * (rows + hid) * width),
    )(*args)


def ring(x, shift, axis="y", n=4):
    return lax.ppermute(x, axis, [(i, (i + shift) % n) for i in range(n)])


def swap(x, axis):
    return ring(x, 1, axis, 2)


def ring_gather(x):
    return [x, ring(x, 1), ring(x, -1), ring(x, 2)]


def after(x, *others):
    return lax.optimization_barrier((x, *others))[0]


def local(grad_out, expert_ids, route_prob, attn_out, w_down, hidden_saved):
    n_experts = lax.axis_size(ALL)
    slots = hidden_saved.shape[1]
    cap = slots // n_experts
    g = grad_out[0]
    width = g.shape[1]
    y = lax.axis_index("y").reshape(1)
    (at_near, near), (at_far, far) = CHUNKS
    ids = expert_ids[0].T
    label = jnp.pad(ids.astype(BF), ((0, g.shape[0] - ids.shape[0]), (0, 0)))
    low = jnp.concatenate([g[:, at_near : at_near + near], label], axis=1)
    across = swap(after(g, low), "zlo")
    low = ring_gather(low)
    spread = place(y, low, slots)
    named = ids[:, None, :] == jnp.arange(n_experts, dtype=jnp.int32)[None, :, None]
    rank = ranks(jnp.any(named, axis=0))
    prob = jnp.sum(jnp.where(named, route_prob[0].T[:, None, :].astype(F32), 0.0), axis=0)
    at = rank[:, None, :] == jnp.arange(cap, dtype=jnp.int32).astype(F32)[None, :, None]
    send_prob = jnp.sum(jnp.where(at, prob[:, None, :], 0.0), axis=2)
    got_prob = lax.all_to_all(
        send_prob.reshape(n_experts, 1, cap), ALL, split_axis=0, concat_axis=0, tiled=True
    )
    high = ring_gather(after(g[:, at_far : at_far + far], send_prob))
    *low, got_prob, across = lax.optimization_barrier((*low, got_prob, across))

    def send(rows):
        return lax.all_to_all(
            rows.reshape(n_experts // 4, 4 * cap, -1), PEERS, split_axis=0, concat_axis=0, tiled=True
        ).reshape(slots, -1)

    rows0 = dispatch(spread, low, near)
    routed0 = send(rows0)
    contexts = after(attn_out, high[3])
    contexts = [contexts, ring(contexts, 1), ring(contexts, -1)]
    parts = quarters(y, across)
    other = [ring(q, shift) if shift else q for q, shift in zip(parts, (0, 1, -1, 2))]
    mine = select(y, low, high, width)
    rows1 = dispatch(spread, high, far)
    routed1 = send(rows1)
    weight = got_prob.reshape(slots, 1)
    hidden = hidden_saved[0]
    hidden_t = hidden.T
    w = w_down[0]
    proj = project(0, routed0, w, None, hidden, weight)
    down = weigh(0, routed0, hidden_t, weight, width, None)

    t = (lax.axis_index("zlo") * 2 + lax.axis_index("core")).reshape(1)
    half = attn_out.shape[0] // 2
    contexts += [ring(contexts[1][:half], 1), ring(contexts[2][half:], -1)]
    *other, proj, down = lax.optimization_barrier((*other, proj, down))
    other = jnp.concatenate(other, axis=0)
    features = [mine, swap(mine, "core"), other, swap(other, "core")]
    partial = outer(t, features, contexts)

    x, zhi = lax.axis_index("x"), lax.axis_index("zhi")
    half, eighth = partial.shape[0] // 2, partial.shape[0] // 8
    come = swap(lax.dynamic_slice_in_dim(partial, (1 - zhi) * half, half, 0), "zhi")
    grad_hid, part = project(1, routed1, w, proj, hidden, weight)
    come = after(come, part)
    sums = lax.dynamic_slice_in_dim(partial, zhi * half, half, 0).astype(F32) + come.astype(F32)

    def piece(shift):
        return lax.dynamic_slice_in_dim(sums, ((x + shift) & 3) * eighth, eighth, 0)

    pieces = [ring(piece(shift).astype(BF), shift, "x") for shift in (1, -1, 2)]
    down = weigh(1, routed1, hidden_t, weight, width, down)
    *pieces, _ = lax.optimization_barrier((*pieces, down))
    total = piece(0)
    for come in pieces:
        total = total + come.astype(F32)
    grad_oproj = total.astype(BF)
    returned = lax.all_to_all(part[:, None, :], ALL, split_axis=0, concat_axis=0, tiled=True)[:, 0, :cap]
    value = jnp.sum(jnp.where(at, returned[:, :, None], 0.0), axis=1)
    grad_prob = jnp.sum(jnp.where(named, value[None], 0.0), axis=1).T[None]
    return (grad_prob, grad_hid[None], down[None], grad_oproj)


def solution(mesh):
    fine = Mesh(mesh.devices.reshape(2, 2, 4, 2, 4), ALL)
    in_specs = (
        P(TP, CP, None),
        P(TP, CP, None),
        P(TP, CP, None),
        P(CP, TP),
        P(ALL, None, None),
        P(ALL, None, None),
    )
    out_specs = (
        P(TP, CP, None),
        P(ALL, None, None),
        P(ALL, None, None),
        P(CP, TP),
    )
    return jax.shard_map(local, mesh=fine, in_specs=in_specs, out_specs=out_specs, check_vma=False)
```

```python
import jax
import jax.numpy as jnp
from jax import lax
from jax.experimental import pallas as pl
from jax.experimental.pallas import tpu as pltpu
from jax.sharding import Mesh
from jax.sharding import PartitionSpec as P

TP = ("zlo", "core")
CP = ("x", "zhi", "y")
ALL = TP + CP
PEERS = ("zlo", "core", "x", "zhi")
CHUNKS = ((2560, 1536), (0, 2560))
TILE = 512
WIDE = 512
VMEM = 56 * 1024 * 1024
BF = jnp.bfloat16
F32 = jnp.float32


def params():
    return pltpu.CompilerParams(vmem_limit_bytes=VMEM)


def cost(flops, moved):
    return pl.CostEstimate(flops=flops, bytes_accessed=moved, transcendentals=0)


def upper(n):
    return (
        lax.broadcasted_iota(jnp.int32, (n, n), 0) < lax.broadcasted_iota(jnp.int32, (n, n), 1)
    ).astype(BF)


def ranks(member):
    count = jnp.dot(member.astype(BF), upper(member.shape[1]), preferred_element_type=F32)
    return jnp.where(member, count, -1.0)


def place_kernel(y_ref, *refs):
    s_ref = refs[-1]
    y = y_ref[0]
    rows, cols = s_ref.shape
    peers = rows // 40
    expert = (lax.broadcasted_iota(jnp.int32, (peers, 128), 0) * 4 + y).astype(F32)
    parts = []
    for ref in refs[:-1]:
        named = ref[...].astype(F32)
        member = named[0:1, :] == expert
        for i in range(1, 8):
            member = member | (named[i : i + 1, :] == expert)
        parts.append(ranks(member).astype(BF))
    table = jnp.concatenate(parts, axis=1)
    row = lax.broadcasted_iota(jnp.int32, (rows, peers), 0)
    peer = lax.broadcasted_iota(jnp.int32, (rows, peers), 1)
    pick = (lax.shift_right_logical(row * 6554, 18) == peer).astype(BF)
    spread = jnp.dot(pick, table, preferred_element_type=F32)
    row = lax.broadcasted_iota(jnp.int32, (rows, cols), 0)
    tenth = lax.shift_right_logical(row * 6554, 16)
    rank = (row - tenth * 10).astype(F32)
    block = lax.shift_right_logical(lax.broadcasted_iota(jnp.int32, (rows, cols), 1), 7)
    origin = jnp.where(block == 0, 0, jnp.where(block == 1, 3, jnp.where(block == 2, 1, 2)))
    here = (tenth & 3) == ((origin + y) & 3)
    s_ref[...] = jnp.where(here & (spread == rank), 1.0, 0.0).astype(BF)


def place(y, blocks, rows):
    last = blocks[0].shape[1] // 128 - 1
    return pl.pallas_call(
        place_kernel,
        out_shape=jax.ShapeDtypeStruct((rows, 512), BF),
        grid=(1,),
        in_specs=[pl.BlockSpec(memory_space=pltpu.SMEM)]
        + [pl.BlockSpec((16, 128), lambda i: (0, last)) for _ in blocks],
        out_specs=pl.BlockSpec((rows, 512), lambda i: (0, 0)),
        compiler_params=params(),
        cost_estimate=cost(10**8, 2 * 10**6),
    )(y, *blocks)


def dispatch_kernel(s_ref, g0, g1, g2, g3, o_ref):
    g = jnp.concatenate([g0[...], g1[...], g2[...], g3[...]], axis=0)
    o_ref[...] = jnp.dot(s_ref[...], g, preferred_element_type=F32).astype(BF)


def dispatch(s, blocks, width, weight=1):
    rows = s.shape[0]
    return pl.pallas_call(
        dispatch_kernel,
        out_shape=jax.ShapeDtypeStruct((rows, width), BF),
        grid=(width // TILE,),
        in_specs=[pl.BlockSpec(s.shape, lambda i: (0, 0))]
        + [pl.BlockSpec((128, TILE), lambda i: (0, i)) for _ in blocks],
        out_specs=pl.BlockSpec((rows, TILE), lambda i: (0, i)),
        compiler_params=params(),
        cost_estimate=cost(2 * rows * 512 * width * weight, 2 * rows * width),
    )(s, *blocks)


def select_kernel(y_ref, *refs):
    out = refs[-1]
    col = 0
    for first, (_, width) in ((4, CHUNKS[1]), (0, CHUNKS[0])):
        for i in range(width // 512):
            at = pl.multiple_of(i * 512 + y_ref[0] * 128, 128)
            for k in range(4):
                out[k * 128 : (k + 1) * 128, col : col + 128] = refs[first + k][:, pl.ds(at, 128)]
            col += 128


def select(y, low, high, width):
    moved = 8 * 128 * width
    return pl.pallas_call(
        select_kernel,
        out_shape=jax.ShapeDtypeStruct((512, width // 4), BF),
        in_specs=[pl.BlockSpec(memory_space=pltpu.SMEM)]
        + [pl.BlockSpec(memory_space=pltpu.VMEM)] * 8,
        out_specs=pl.BlockSpec(memory_space=pltpu.VMEM),
        compiler_params=params(),
        cost_estimate=cost(0, moved),
    )(y, *low, *high)


def quarter_kernel(y_ref, g_ref, *outs):
    for out, shift in zip(outs, (0, 1, 3, 2)):
        y = (y_ref[0] + shift) & 3
        for i in range(g_ref.shape[1] // 512):
            at = pl.multiple_of(i * 512 + y * 128, 128)
            out[:, i * 128 : (i + 1) * 128] = g_ref[:, pl.ds(at, 128)]


def quarters(y, g):
    return pl.pallas_call(
        quarter_kernel,
        out_shape=[jax.ShapeDtypeStruct((128, g.shape[1] // 4), BF)] * 4,
        in_specs=[pl.BlockSpec(memory_space=pltpu.SMEM), pl.BlockSpec(memory_space=pltpu.VMEM)],
        out_specs=[pl.BlockSpec(memory_space=pltpu.VMEM)] * 4,
        compiler_params=params(),
        cost_estimate=cost(0, 4 * g.shape[0] * g.shape[1]),
    )(y, g)


def outer_kernel(t_ref, *refs):
    features, contexts, (o_ref, ft, at) = refs[:4], refs[4:9], refs[9:]

    @pl.when(pl.program_id(0) == 0)
    def _():
        for i, f in enumerate(features):
            turned = f[...].T
            for j in range(8):
                to, of = (j % 2 * 4 + j // 2) * 128, j * 128
                ft[to : to + 128, i * 512 : (i + 1) * 512] = turned[of : of + 128]

    for i in range(4):
        who = t_ref[0] ^ i
        start = pl.multiple_of(who * 128, 128)
        for k in range(3):
            at[(i * 4 + k) * 128 : (i * 4 + k + 1) * 128, :] = contexts[k][pl.ds(start, 128), :]
        start = pl.multiple_of((who & 1) * 128, 128)
        at[(i * 4 + 3) * 128 : (i * 4 + 4) * 128, :] = jnp.where(
            who < 2, contexts[3][pl.ds(start, 128), :], contexts[4][pl.ds(start, 128), :]
        )
    o_ref[...] = jnp.dot(ft[...], at[...], preferred_element_type=F32).astype(BF)


def outer(t, features, contexts):
    n, wide = features[0].shape[1], contexts[0].shape[1]
    return pl.pallas_call(
        outer_kernel,
        out_shape=jax.ShapeDtypeStruct((n, wide), BF),
        grid=(wide // 256,),
        in_specs=[pl.BlockSpec(memory_space=pltpu.SMEM)]
        + [pl.BlockSpec((512, n), lambda i: (0, 0)) for _ in features]
        + [pl.BlockSpec((c.shape[0], 256), lambda i: (0, i)) for c in contexts],
        out_specs=pl.BlockSpec((n, 256), lambda i: (0, i)),
        scratch_shapes=[pltpu.VMEM((n, 2048), BF), pltpu.VMEM((2048, 256), BF)],
        compiler_params=params(),
        cost_estimate=cost(2 * 2048 * n * wide, 2 * (4096 * n + n * wide)),
    )(t, *features, *contexts)


def proj_kernel(first, last, *refs):
    routed_ref, *refs = refs
    term = None
    tile = refs[0].shape[1]
    for i in range(routed_ref.shape[1] // tile):
        piece = lax.dot_general(
            routed_ref[:, i * tile : (i + 1) * tile],
            refs.pop(0)[...],
            (((1,), (1,)), ((), ())),
            preferred_element_type=F32,
        )
        term = piece if term is None else term + piece
    if not first:
        term = refs[0][...] + term
    if not last:
        refs[-1][...] = term
        return
    h_ref, wt_ref, hid_ref, part_ref = refs[-4:]
    hid_ref[...] = (wt_ref[...] * term).astype(BF)
    part = jnp.sum(term * h_ref[...].astype(F32), axis=1, keepdims=True)
    rows, peers = part.shape[0], part_ref.shape[0]
    row = lax.broadcasted_iota(jnp.int32, (rows, 128), 0)
    lane = lax.broadcasted_iota(jnp.int32, (rows, 128), 1)
    tenth = lax.shift_right_logical(row * 6554, 16)
    spread = jnp.where(lane == row - tenth * 10, part, 0.0)
    peer = lax.broadcasted_iota(jnp.int32, (peers, rows), 0)
    col = lax.shift_right_logical(lax.broadcasted_iota(jnp.int32, (peers, rows), 1) * 6554, 16)
    part_ref[...] = jnp.dot(
        (peer == col).astype(F32), spread, precision=lax.Precision.HIGHEST, preferred_element_type=F32
    )


def project(chunk, routed, w, before, hidden, weight):
    rows, width = routed.shape
    hid = w.shape[0]
    first, last = chunk == 0, chunk == len(CHUNKS) - 1
    tile = 640
    across = pl.BlockSpec((tile, hid), lambda i: (i, 0))
    narrow = pl.BlockSpec((tile, 1), lambda i: (i, 0))
    deep = WIDE if CHUNKS[chunk][0] else width
    start, n = CHUNKS[chunk][0] // deep, width // deep
    in_specs = [pl.BlockSpec((tile, width), lambda i: (i, 0))]
    in_specs += [pl.BlockSpec((hid, deep), lambda i, j=j: (0, j)) for j in range(start, start + n)]
    args = [routed] + [w] * n
    if not first:
        in_specs.append(across)
        args.append(before)
    if last:
        in_specs += [across, narrow]
        args += [hidden, weight]
        out_shape = [jax.ShapeDtypeStruct((rows, hid), BF), jax.ShapeDtypeStruct((rows // 10, 128), F32)]
        out_specs = [across, pl.BlockSpec((tile // 10, 128), lambda i: (i, 0))]
    else:
        out_shape, out_specs = jax.ShapeDtypeStruct((rows, hid), F32), across

    def kernel(*refs):
        proj_kernel(first, last, *refs)

    return pl.pallas_call(
        kernel,
        out_shape=out_shape,
        grid=(rows // tile,),
        in_specs=in_specs,
        out_specs=out_specs,
        compiler_params=params(),
        cost_estimate=cost(2 * rows * hid * width, 2 * (rows + hid) * width),
    )(*args)


def down_kernel(routed_ref, ht_ref, wt_ref, *refs):
    weighted = (wt_ref[...] * routed_ref[...].astype(F32)).astype(BF)
    refs[-1][...] = jnp.dot(ht_ref[...], weighted, preferred_element_type=F32).astype(BF)


def weigh(chunk, routed, hidden_t, weight, full, before):
    rows, width = routed.shape
    hid = hidden_t.shape[0]
    tile = width // 2 if width % 256 == 0 and CHUNKS[chunk][0] == 0 else WIDE
    steps = width // tile
    base = CHUNKS[chunk][0] // tile
    in_specs = [
        pl.BlockSpec((rows, tile), lambda i: (0, i)),
        pl.BlockSpec((hid, rows), lambda i: (0, 0)),
        pl.BlockSpec((rows, 1), lambda i: (0, 0)),
    ]
    args = [routed, hidden_t, weight]
    if before is not None:
        in_specs.append(pl.BlockSpec(memory_space=pl.ANY))
        args.append(before)
    return pl.pallas_call(
        down_kernel,
        out_shape=jax.ShapeDtypeStruct((hid, full), BF),
        grid=(steps,),
        in_specs=in_specs,
        out_specs=pl.BlockSpec((hid, tile), lambda i: (0, base + i)),
        input_output_aliases={} if before is None else {3: 0},
        compiler_params=params(),
        cost_estimate=cost(2 * rows * hid * width, 2 * (rows + hid) * width),
    )(*args)


def ring(x, shift, axis="y", n=4):
    return lax.ppermute(x, axis, [(i, (i + shift) % n) for i in range(n)])


def swap(x, axis):
    return ring(x, 1, axis, 2)


def ring_gather(x):
    return [x, ring(x, 1), ring(x, -1), ring(x, 2)]


def after(x, *others):
    return lax.optimization_barrier((x, *others))[0]


def local(grad_out, expert_ids, route_prob, attn_out, w_down, hidden_saved):
    n_experts = lax.axis_size(ALL)
    slots = hidden_saved.shape[1]
    cap = slots // n_experts
    g = grad_out[0]
    width = g.shape[1]
    y = lax.axis_index("y").reshape(1)
    (at_near, near), (at_far, far) = CHUNKS
    ids = expert_ids[0].T
    label = jnp.pad(ids.astype(BF), ((0, g.shape[0] - ids.shape[0]), (0, 0)))
    low = jnp.concatenate([g[:, at_near : at_near + near], label], axis=1)
    across = swap(after(g, low), "zlo")
    low = ring_gather(low)
    spread = place(y, low, slots)
    named = ids[:, None, :] == jnp.arange(n_experts, dtype=jnp.int32)[None, :, None]
    rank = ranks(jnp.any(named, axis=0))
    prob = jnp.sum(jnp.where(named, route_prob[0].T[:, None, :].astype(F32), 0.0), axis=0)
    at = rank[:, None, :] == jnp.arange(cap, dtype=jnp.int32).astype(F32)[None, :, None]
    send_prob = jnp.sum(jnp.where(at, prob[:, None, :], 0.0), axis=2)
    got_prob = lax.all_to_all(
        send_prob.reshape(n_experts, 1, cap), ALL, split_axis=0, concat_axis=0, tiled=True
    )
    high = ring_gather(after(g[:, at_far : at_far + far], send_prob))
    *low, got_prob, across = lax.optimization_barrier((*low, got_prob, across))

    def send(rows):
        return lax.all_to_all(
            rows.reshape(n_experts // 4, 4 * cap, -1), PEERS, split_axis=0, concat_axis=0, tiled=True
        ).reshape(slots, -1)

    rows0 = dispatch(spread, low, near)
    routed0 = send(rows0)
    contexts = after(attn_out, high[3])
    contexts = [contexts, ring(contexts, 1), ring(contexts, -1)]
    parts = quarters(y, across)
    other = [ring(q, shift) if shift else q for q, shift in zip(parts, (0, 1, -1, 2))]
    mine = select(y, low, high, width)
    rows1 = dispatch(spread, high, far)
    routed1 = send(rows1)
    weight = got_prob.reshape(slots, 1)
    hidden = hidden_saved[0]
    hidden_t = hidden.T
    w = w_down[0]
    proj = project(0, routed0, w, None, hidden, weight)
    down = weigh(0, routed0, hidden_t, weight, width, None)

    t = (lax.axis_index("zlo") * 2 + lax.axis_index("core")).reshape(1)
    half = attn_out.shape[0] // 2
    contexts += [ring(contexts[1][:half], 1), ring(contexts[2][half:], -1)]
    *other, proj, down = lax.optimization_barrier((*other, proj, down))
    other = jnp.concatenate(other, axis=0)
    features = [mine, swap(mine, "core"), other, swap(other, "core")]
    partial = outer(t, features, contexts)

    x, zhi = lax.axis_index("x"), lax.axis_index("zhi")
    half, eighth = partial.shape[0] // 2, partial.shape[0] // 8
    come = swap(lax.dynamic_slice_in_dim(partial, (1 - zhi) * half, half, 0), "zhi")
    grad_hid, part = project(1, routed1, w, proj, hidden, weight)
    come = after(come, part)
    sums = lax.dynamic_slice_in_dim(partial, zhi * half, half, 0).astype(F32) + come.astype(F32)

    def piece(shift):
        return lax.dynamic_slice_in_dim(sums, ((x + shift) & 3) * eighth, eighth, 0)

    pieces = [ring(piece(shift).astype(BF), shift, "x") for shift in (1, -1, 2)]
    down = weigh(1, routed1, hidden_t, weight, width, down)
    *pieces, _ = lax.optimization_barrier((*pieces, down))
    total = piece(0)
    for come in pieces:
        total = total + come.astype(F32)
    grad_oproj = total.astype(BF)
    returned = lax.all_to_all(part[:, None, :], ALL, split_axis=0, concat_axis=0, tiled=True)[:, 0, :cap]
    value = jnp.sum(jnp.where(at, returned[:, :, None], 0.0), axis=1)
    grad_prob = jnp.sum(jnp.where(named, value[None], 0.0), axis=1).T[None]
    return (grad_prob, grad_hid[None], down[None], grad_oproj)


def solution(mesh):
    fine = Mesh(mesh.devices.reshape(2, 2, 4, 2, 4), ALL)
    in_specs = (
        P(TP, CP, None),
        P(TP, CP, None),
        P(TP, CP, None),
        P(CP, TP),
        P(ALL, None, None),
        P(ALL, None, None),
    )
    out_specs = (
        P(TP, CP, None),
        P(ALL, None, None),
        P(ALL, None, None),
        P(CP, TP),
    )
    return jax.shard_map(local, mesh=fine, in_specs=in_specs, out_specs=out_specs, check_vma=False)
```
